768 devices in a mesh: row: 24 (over z_hi, y), col: 32 (over z_lo, x, core).
Axes of the slice: x: 4, y: 8, z: 12 (z_hi: 3, z_lo: 4; z = z_hi * 4 + z_lo), core: 2. Of those that a mesh axis runs over, the one named last changes fastest.
Arguments:
- density: float32 [1536, 9, 128, 128], P(('row', 'col')), may hold values from -0.1 to 0.6, as said below
- band_mask: int32 [1536, 9], P(('row', 'col')), may hold values 0 or 1
Outputs:
- purified: float32 [1536, 9, 128, 128], P(('row', 'col'))
The draws below stay inside these ranges and needn't reach their ends.
Inputs may be any that keep to these rules, and one draw needn't show every extreme that they name: `density`: blocks on the main block diagonal are one half times the identity plus small entries; other blocks are small.
All inputs are finite; a program needn't handle non-finite values. No bound on the sum of `band_mask` on one device may be relied on, other than what follows from the above.
Results may differ from the reference program's by a relative error of at most 0.0003.
Values sent between devices are 32-bit elements; how exact they have to be, the bound alone decides.
A program may use at most 32 MiB of HBM per device.

```python
import jax
import jax.numpy as jnp
from jax import lax

BLK = 128
W = 4
K = 9
BROWS = 2
NB = 1536


def draw_density(key, part):
    key = jax.random.fold_in(key, 11)
    noise_key = jax.random.fold_in(key, 0)
    sigma = 0.015
    noise = jnp.clip(jax.random.normal(noise_key, (NB, K, BLK, BLK), jnp.float32) * sigma, -0.09, 0.09)
    diagonal = (jnp.arange(K)[:, None, None] == W) * jnp.eye(BLK, dtype=jnp.float32)[None, :, :] * 0.5
    return (noise + diagonal[None, :, :, :]).astype(jnp.float32)


def set_ends(entries, stream_key, least, top_value):
    index_at = [jax.random.randint(jax.random.fold_in(stream_key, axis), (), 0, length) for axis, length in enumerate(entries.shape)]
    main_axis = entries.shape.index(max(entries.shape))
    next_to = index_at[:main_axis] + [(index_at[main_axis] + 1) % entries.shape[main_axis]] + index_at[main_axis + 1:]
    return entries.at[tuple(index_at)].set(least).at[tuple(next_to)].set(top_value)


def setup_inputs(seed: int = 0) -> dict:
    seeds = jax.random.split(jax.random.key(seed), 3)
    return {
        "density": draw_density(jax.random.fold_in(seeds[2], 71), 0),
        "band_mask": set_ends((jax.random.randint(seeds[1], (NB, K), 0, 4) < 3).astype(jnp.int32), jax.random.fold_in(seeds[1], 1), 0, 1),
    }


def band_product(left_rows, right_pad):
    row_count = left_rows.shape[0]
    diagonals = left_rows.shape[1]
    half_width = (diagonals - 1) // 2
    total = jnp.zeros(left_rows.shape, jnp.float32)
    for offset in range(diagonals):
        lowest = max(0, half_width - offset)
        highest = min(2 * half_width, 3 * half_width - offset)
        number = highest - lowest + 1
        start = lowest + offset - half_width
        right_rows = right_pad[offset:offset + row_count, lowest:highest + 1]
        product = jnp.einsum("ixy,ifyz->ifxz", left_rows[:, offset], right_rows, precision=lax.Precision.HIGHEST)
        total = total + jnp.pad(product, ((0, 0), (start, diagonals - start - number), (0, 0), (0, 0)))
    return total


def reference(density, band_mask):
    mask_float = band_mask.astype(jnp.float32)[:, :, None, None]
    masked = density * mask_float
    groups = NB // BROWS

    def one_group(group):
        row_index = (group * BROWS - W + jnp.arange(BROWS + 2 * W, dtype=jnp.int32)) % NB
        padded = jnp.take(masked, row_index.astype(jnp.int32), axis=0)
        local_rows = padded[W:W + BROWS]
        mask_rows = lax.dynamic_slice_in_dim(mask_float, (group * BROWS).astype(jnp.int32), BROWS, 0)
        square = band_product(local_rows, padded)
        cube = band_product(square, padded)
        return (3.0 * square - 2.0 * cube) * mask_rows

    result = lax.map(one_group, jnp.arange(groups, dtype=jnp.int32))
    return result.reshape((NB, K, BLK, BLK))
```

```python
import functools

import jax
import jax.numpy as jnp
from jax import lax
from jax.experimental import pallas as pl
from jax.experimental.pallas import tpu as pltpu
from jax.sharding import PartitionSpec as P

MESH = pl.DeviceIdType.MESH
F32, BF16 = jnp.float32, jnp.bfloat16
BLK = 128
K = 9
SLOTS = 2 * K
TILE = 2 * BLK

NEAR_SLOW = ((0, 4, 5), (1, 3, 6)), ((0, 2, 2), (1, 1, 2))
NEAR_FAST = ((0, 0, 6), (1, 0, 5)), ((0, 6, 2), (1, 5, 2))
FAR_SLOW = ((0, 8, 1), (1, 7, 2)), ((0, 6, 2), (1, 5, 2)), ((0, 4, 2), (1, 3, 2))
FAR_FAST = (((0, 0, 6), (1, 0, 5)),)


def kernel(rows, cols, x_ref, mask_ref, out_ref, held, marks, high, low, s_high, s_low, square, cube, send, recv, local_sem):
    core = lax.rem(lax.axis_index("col"), 2)
    g = lax.axis_index("row") * cols + lax.axis_index("col")

    def device(index):
        index = lax.rem(index + rows * cols, rows * cols)
        return lax.div(index, cols), lax.rem(index, cols)

    slow, fast = device(g + 2 * core - 1), device(g + 1 - 2 * core)

    barrier = pltpu.get_barrier_semaphore()
    for other in (slow, fast):
        pl.semaphore_signal(barrier, inc=1, device_id=other, device_id_type=MESH)

    own = pltpu.make_async_copy(x_ref, held.at[2], local_sem)
    own.start()
    for s in range(SLOTS):
        value = mask_ref[s // K, s % K].astype(F32)
        marks[2, s : s + 1, :] = jnp.full((1, BLK), value, F32)

    def entry(row, d):
        s = row * K + d
        return jnp.where(core == 0, s, SLOTS - 1 - s)

    def span(piece):
        row, d, count = piece
        s = row * K + d
        return pl.ds(jnp.where(core == 0, s, SLOTS - s - count), count)

    def corner(row, d):
        e = d + row
        r, c = jnp.where(core == 0, row, 1 - row), jnp.where(core == 0, e % 2, 1 - e % 2)
        return (
            e // 2 - 2,
            pl.ds(pl.multiple_of(r * BLK, BLK), BLK),
            pl.ds(pl.multiple_of(c * BLK, BLK), BLK),
        )

    for j in range(3):
        for row, d, k in ((0, K, j + 2), (1, -1, j)):
            _, r, c = corner(row, d)
            at = j if row == 0 else j + 2
            high[at, k, r, c] = jnp.zeros((BLK, BLK), BF16)
            low[at, k, r, c] = jnp.zeros((BLK, BLK), BF16)

    pl.semaphore_wait(barrier, 2)

    started = []

    def start(source, target, number, to):
        copy = pltpu.make_async_remote_copy(
            src_ref=source,
            dst_ref=target,
            send_sem=send.at[number],
            recv_sem=recv.at[number],
            device_id=to,
            device_id_type=MESH,
        )
        copy.start()
        started.append(copy)

    def landed(target, number):
        pltpu.make_async_remote_copy(
            src_ref=target,
            dst_ref=target,
            send_sem=send.at[number],
            recv_sem=recv.at[number],
            device_id=slow,
            device_id_type=MESH,
        ).wait_recv()

    def mirrored(piece):
        row, d, count = piece
        return 1 - row, K - d - count, count

    def give(source, at, pieces, number, to):
        for i, piece in enumerate(pieces):
            part = span(mirrored(piece))
            start(source.at[part], held.at[at, part], number + i, to)

    def take(at, pieces, number):
        for i, piece in enumerate(pieces):
            landed(held.at[at, span(piece)], number + i)

    start(marks.at[2], marks.at[1], 0, slow)
    start(marks.at[2], marks.at[3], 5, fast)
    give(x_ref, 1, NEAR_SLOW[0], 1, slow)
    give(x_ref, 3, NEAR_FAST[0], 6, fast)
    give(x_ref, 1, NEAR_SLOW[1], 3, slow)
    give(x_ref, 3, NEAR_FAST[1], 8, fast)

    def split(at, pieces):
        for row, first, count in pieces:
            def one(d, carry, row=row):
                s = entry(row, d)
                k, r, c = corner(row, d)
                value = held[at, s] * marks[at, pl.ds(s, 1), :]
                top = value.astype(BF16)
                high[at, at + k, r, c] = top
                low[at, at + k, r, c] = (value - top.astype(F32)).astype(BF16)
                return carry

            lax.fori_loop(first, first + count, one, 0)

    def product(a_high, a_low, j, k):
        b_high, b_low = high[j, k], low[j, k]
        dot = functools.partial(jnp.dot, preferred_element_type=F32)
        return dot(a_high, b_high) + (dot(a_high, b_low) + dot(a_low, b_high))

    def square_row(j, first, last, fresh=False):
        def one(k, carry):
            term = product(high[2, j], low[2, j], j, k)
            square[k] = term if fresh else square[k] + term
            return carry

        lax.fori_loop(first, last + 1, one, 0, unroll=True)

    def cube_row(j, first, last):
        def one(k, carry):
            cube[k] = cube[k] + product(s_high[j], s_low[j], j, k)
            return carry

        lax.fori_loop(first, last + 1, one, 0, unroll=True)

    def finish_square(j):
        if j in (0, 4):
            _, r, c = corner(*((1, -1) if j == 0 else (0, K)))
            square[j, r, c] = jnp.zeros((BLK, BLK), F32)
        value = square[j]
        top = value.astype(BF16)
        s_high[j] = top
        s_low[j] = (value - top.astype(F32)).astype(BF16)

    own.wait()
    split(2, ((0, 0, K), (1, 0, K)))
    cube[...] = jnp.zeros_like(cube)
    square_row(2, 0, 4, fresh=True)

    landed(marks.at[3], 5)
    start(marks.at[3], marks.at[0], 10, slow)
    take(3, NEAR_FAST[0], 6)
    for i, pieces in enumerate(FAR_SLOW):
        give(held.at[3], 0, pieces, 11 + 2 * i, slow)
    take(3, NEAR_FAST[1], 8)
    split(3, ((0, 0, 8), (1, 0, 7)))
    square_row(3, 1, 4)

    landed(marks.at[1], 0)
    start(marks.at[1], marks.at[4], 17, fast)
    take(1, NEAR_SLOW[0], 1)
    give(held.at[1], 4, FAR_FAST[0], 18, fast)
    split(1, NEAR_SLOW[0])
    square_row(1, 1, 3)
    take(1, NEAR_SLOW[1], 3)
    split(1, NEAR_SLOW[1])
    square_row(1, 0, 0)

    landed(marks.at[4], 17)
    take(4, FAR_FAST[0], 18)
    split(4, FAR_FAST[0])
    square_row(4, 2, 4)
    finish_square(4)
    cube_row(4, 2, 4)
    finish_square(3)
    cube_row(3, 1, 4)

    landed(marks.at[0], 10)
    for i, pieces in enumerate(FAR_SLOW):
        take(0, pieces, 11 + 2 * i)
        split(0, pieces)
        k = 2 - i
        square_row(0, k, k)
        finish_square(k)
        cube_row(k, 0, k + 2)

    for row in range(2):
        def one(d, carry, row=row):
            s = entry(row, d)
            k, r, c = corner(row, d)
            value = 3.0 * square[k + 2, r, c] - 2.0 * cube[k + 2, r, c]
            out_ref[s] = value * marks[2, pl.ds(s, 1), :]
            return carry

        lax.fori_loop(0, K, one, 0)

    for copy in started:
        copy.wait_send()


def solution(mesh):
    rows, cols = mesh.shape["row"], mesh.shape["col"]

    def local(density, band_mask):
        result = pl.pallas_call(
            functools.partial(kernel, rows, cols),
            out_shape=jax.ShapeDtypeStruct((SLOTS, BLK, BLK), F32),
            in_specs=[
                pl.BlockSpec(memory_space=pltpu.HBM),
                pl.BlockSpec(memory_space=pltpu.SMEM),
            ],
            out_specs=pl.BlockSpec(memory_space=pltpu.VMEM),
            scratch_shapes=[
                pltpu.VMEM((5, SLOTS, BLK, BLK), F32),
                pltpu.VMEM((5, 24, BLK), F32),
                pltpu.VMEM((5, 5, TILE, TILE), BF16),
                pltpu.VMEM((5, 5, TILE, TILE), BF16),
                pltpu.VMEM((5, TILE, TILE), BF16),
                pltpu.VMEM((5, TILE, TILE), BF16),
                pltpu.VMEM((5, TILE, TILE), F32),
                pltpu.VMEM((5, TILE, TILE), F32),
                pltpu.SemaphoreType.DMA((20,)),
                pltpu.SemaphoreType.DMA((20,)),
                pltpu.SemaphoreType.DMA,
            ],
            compiler_params=pltpu.CompilerParams(
                collective_id=0, has_side_effects=True, vmem_limit_bytes=40 << 20
            ),
        )(pltpu.with_memory_space_constraint(density.reshape(SLOTS, BLK, BLK), pltpu.HBM), band_mask)
        return result.reshape(density.shape)

    return jax.shard_map(
        local,
        mesh=mesh,
        in_specs=(P(("row", "col"), None, None, None), P(("row", "col"), None)),
        out_specs=P(("row", "col"), None, None, None),
        check_vma=False,
    )
```

```python
import functools

import jax
import jax.numpy as jnp
from jax import lax
from jax.experimental import pallas as pl
from jax.experimental.pallas import tpu as pltpu
from jax.sharding import PartitionSpec as P

MESH = pl.DeviceIdType.MESH
F32, BF16 = jnp.float32, jnp.bfloat16
BLK = 128
K = 9
SLOTS = 2 * K
TILE = 2 * BLK

NEAR_SLOW = (
    ((0, 8, 1), (1, 7, 2)),
    ((0, 6, 2), (1, 5, 2)),
    ((0, 4, 2), (1, 3, 2)),
    ((0, 2, 2), (1, 1, 2)),
)
NEAR_FAST = ((0, 0, 6), (1, 0, 5)), ((0, 6, 2), (1, 5, 2))
FAR = ((0, 8, 1), (1, 7, 2)), ((0, 6, 2), (1, 5, 2)), ((0, 5, 1), (1, 4, 1)), ((0, 4, 1), (1, 3, 1))

MARKS_SLOW, MARKS_FAST, MARKS_FAR = 0, 1, 2
AT_SLOW, AT_FAST, AT_FAR, SEMAPHORES = 4, 12, 16, 32


def kernel(rows, cols, x_ref, mask_ref, out_ref, held, masks, marks, high, low, s_high, s_low, square, cube, send, recv, local_sem, ready):
    core = lax.rem(lax.axis_index("col"), 2)
    g = lax.axis_index("row") * cols + lax.axis_index("col")

    def device(index):
        index = lax.rem(index + rows * cols, rows * cols)
        return lax.div(index, cols), lax.rem(index, cols)

    slow, fast = device(g + 2 * core - 1), device(g + 1 - 2 * core)

    barrier = pltpu.get_barrier_semaphore()
    pl.semaphore_signal(barrier, inc=1, device_id=slow, device_id_type=MESH)

    @pl.when(core == 1)
    def _():
        pl.semaphore_signal(barrier, inc=1, device_id=fast, device_id_type=MESH)

    own = pltpu.make_async_copy(x_ref, held.at[2], local_sem.at[0])
    own_mask = pltpu.make_async_copy(mask_ref, masks.at[2], local_sem.at[1])
    own.start()
    own_mask.start()

    def entry(flip, row, d):
        s = row * K + d
        return jnp.where(flip == 0, s, SLOTS - 1 - s)

    def span(flip, piece):
        row, d, count = piece
        s = row * K + d
        return pl.ds(jnp.where(flip == 0, s, SLOTS - s - count), count)

    def half(flip, r):
        return pl.ds(pl.multiple_of(jnp.where(flip == 0, r, 1 - r) * BLK, BLK), BLK)

    def place(flip, row, d):
        e = d + row
        return e // 2 - 2, half(flip, row), half(flip, e % 2)

    started = []

    def start(source, target, number, to):
        copy = pltpu.make_async_remote_copy(
            src_ref=source,
            dst_ref=target,
            send_sem=send.at[number],
            recv_sem=recv.at[number],
            device_id=to,
            device_id_type=MESH,
        )
        copy.start()
        started.append(copy)

    def landed(target, number):
        pltpu.make_async_remote_copy(
            src_ref=target,
            dst_ref=target,
            send_sem=send.at[number],
            recv_sem=recv.at[number],
            device_id=slow,
            device_id_type=MESH,
        ).wait_recv()

    def give(source, at, flip, pieces, number, to):
        for i, piece in enumerate(pieces):
            part = span(flip, piece)
            start(source.at[part], held.at[at, part], number + i, to)

    def take(at, flip, pieces, number):
        for i, piece in enumerate(pieces):
            landed(held.at[at, span(flip, piece)], number + i)

    pl.semaphore_wait(barrier, 2 - core)

    @pl.when(core == 0)
    def _():
        pl.semaphore_signal(ready, inc=1, device_id=fast, device_id_type=MESH)

    start(mask_ref, masks.at[1], MARKS_SLOW, slow)
    for i, pieces in enumerate(NEAR_SLOW):
        give(x_ref, 1, 1 - core, pieces, AT_SLOW + 2 * i, slow)

    for j in range(3):
        for row, d, at, k in ((0, K, j, j + 2), (1, -1, j + 2, j)):
            _, r, c = place(core, row, d)
            high[at, k, r, c] = jnp.zeros((BLK, BLK), BF16)
            low[at, k, r, c] = jnp.zeros((BLK, BLK), BF16)
    cube[...] = jnp.zeros_like(cube)

    def mark(at):
        value = masks[at].astype(F32)
        for s in range(SLOTS):
            one = value[s // K : s // K + 1, s % K : s % K + 1]
            marks[at, s : s + 1, :] = jnp.broadcast_to(one, (1, BLK))

    def split(at, flip, pieces, turned=None):
        for row, first, count in pieces:
            def one(d, carry, row=row):
                s = entry(flip, row, d)
                k, r, c = place(flip, row, d)
                value = held[at, s] * marks[at, pl.ds(s, 1), :]
                top = value.astype(BF16)
                k = at + k if turned is None else turned(k)
                high[at, k, r, c] = top
                low[at, k, r, c] = (value - top.astype(F32)).astype(BF16)
                return carry

            lax.fori_loop(first, first + count, one, 0)

    dot = functools.partial(jnp.dot, preferred_element_type=F32)

    def product(a_high, a_low, b_high, b_low):
        return dot(a_high, b_high) + (dot(a_high, b_low) + dot(a_low, b_high))

    def square_row(j, tiles, fresh=False):
        for k in tiles:
            term = product(high[2, j], low[2, j], high[j, k], low[j, k])
            square[k] = term if fresh else square[k] + term

    def cube_row(j, tiles):
        for k in tiles:
            cube[k] = cube[k] + product(s_high[j], s_low[j], high[j, k], low[j, k])

    def finish_square(j, r=slice(None), c=slice(None)):
        value = square[j, r, c]
        top = value.astype(BF16)
        s_high[j, r, c] = top
        s_low[j, r, c] = (value - top.astype(F32)).astype(BF16)

    def give_out(flip, pieces, tile):
        for row, first, count in pieces:
            def one(d, carry, row=row):
                s = entry(flip, row, d)
                k, r, c = place(flip, row, d)
                k = tile(k + 2)
                value = 3.0 * square[k, r, c] - 2.0 * cube[k, r, c]
                out_ref[s] = value * marks[2, pl.ds(s, 1), :]
                return carry

            lax.fori_loop(first, first + count, one, 0)

    own.wait()
    own_mask.wait()
    mark(2)
    split(2, core, ((0, 0, K), (1, 0, K)))

    @pl.when(core == 1)
    def _():
        pl.semaphore_wait(ready, 1)

    start(mask_ref, masks.at[3], MARKS_FAST, fast)
    for i, pieces in enumerate(NEAR_FAST):
        give(x_ref, 3, 1 - core, pieces, AT_FAST + 2 * i, fast)
    square_row(2, range(5), fresh=True)

    landed(masks.at[3], MARKS_FAST)
    start(masks.at[3], masks.at[0], MARKS_FAR, slow)
    take(3, core, NEAR_FAST[0], AT_FAST)
    for i, pieces in enumerate(FAR):
        give(held.at[3], 0, 1 - core, pieces, AT_FAR + 2 * i, slow)
    take(3, core, NEAR_FAST[1], AT_FAST + 2)
    mark(3)
    split(3, core, ((0, 0, 8), (1, 0, 7)))
    square_row(3, (1, 2, 3, 4))

    landed(masks.at[1], MARKS_SLOW)
    start(masks.at[1], masks.at[4], MARKS_FAR + 1, fast)
    mark(1)
    for i, pieces in enumerate(NEAR_SLOW):
        take(1, core, pieces, AT_SLOW + 2 * i)
        if i < 2:
            give(held.at[1], 4, core, pieces, AT_FAR + 8 + 2 * i, fast)
        elif i == 2:
            for n, part in enumerate(FAR[2:]):
                give(held.at[1], 4, core, part, AT_FAR + 12 + 2 * n, fast)
        split(1, core, pieces)
        square_row(1, (3 - i,))

    for last in (False, True):
        side = jnp.where((g == 1) == last, 1, 0)
        flip = jnp.where(side == 0, core, 1 - core)

        def tile(k, side=side):
            return jnp.where(side == 0, k, 4 - k)

        far = tile(0)
        number = AT_FAR + 8 * side
        landed(masks.at[far], MARKS_FAR + side)
        mark(far)
        for i, pieces in enumerate(FAR):
            take(far, flip, pieces, number + 2 * i)
            split(far, flip, pieces, turned=lambda k: tile(k))
            if i == 0:
                square_row(far, (2,))
                if last:
                    finish_square(2)
                    cube_row(2, range(5))
            elif i == 1:
                square_row(far, (tile(1),))
                finish_square(tile(1))
                cube_row(tile(1), [tile(k) for k in range(4)])
            elif i == 2:
                r0, r1 = half(flip, 0), half(flip, 1)
                c0, c1 = r0, r1
                everything = slice(None)
                square[far, :, c1] += product(high[2, far], low[2, far], high[far, far, :, c1], low[far, far, :, c1])
                finish_square(far, everything, c1)
                a_high, a_low = s_high[far, :, c1], s_low[far, :, c1]
                for k in (tile(1), tile(2)):
                    cube[k] += product(a_high, a_low, high[far, k, c1, :], low[far, k, c1, :])
                cube[far, :, c1] += product(a_high, a_low, high[far, far, c1, c1], low[far, far, c1, c1])
                if last:
                    give_out(flip, ((0, 5, 4), (1, 0, K)), tile)
            else:
                square[far, r0, c0] += product(high[2, far, r0, :], low[2, far, r0, :], high[far, far, :, c0], low[far, far, :, c0])
                finish_square(far, r0, c0)
                a_high, a_low = s_high[far, r0, c0], s_low[far, r0, c0]
                cube[far, r0, c0] += product(s_high[far, r0, :], s_low[far, r0, :], high[far, far, :, c0], low[far, far, :, c0])
                cube[far, r0, c1] += product(a_high, a_low, high[far, far, c0, c1], low[far, far, c0, c1])
                k = tile(1)
                cube[k, r0, :] += product(a_high, a_low, high[far, k, c0, :], low[far, k, c0, :])
                cube[2, r0, c0] += product(a_high, a_low, high[far, 2, c0, c0], low[far, 2, c0, c0])
                if last:
                    give_out(flip, ((0, 0, 5),), tile)

    for copy in started:
        copy.wait_send()


def solution(mesh):
    rows, cols = mesh.shape["row"], mesh.shape["col"]

    def local(density, band_mask):
        blocks = pltpu.with_memory_space_constraint(
            density.reshape(SLOTS, BLK, BLK), pltpu.HBM
        )
        mask = pltpu.with_memory_space_constraint(band_mask, pltpu.HBM)
        result = pl.pallas_call(
            functools.partial(kernel, rows, cols),
            out_shape=jax.ShapeDtypeStruct((SLOTS, BLK, BLK), F32),
            in_specs=[
                pl.BlockSpec(memory_space=pltpu.HBM),
                pl.BlockSpec(memory_space=pltpu.HBM),
            ],
            out_specs=pl.BlockSpec(memory_space=pltpu.VMEM),
            scratch_shapes=[
                pltpu.VMEM((5, SLOTS, BLK, BLK), F32),
                pltpu.VMEM((5, 2, K), jnp.int32),
                pltpu.VMEM((5, 24, BLK), F32),
                pltpu.VMEM((5, 5, TILE, TILE), BF16),
                pltpu.VMEM((5, 5, TILE, TILE), BF16),
                pltpu.VMEM((5, TILE, TILE), BF16),
                pltpu.VMEM((5, TILE, TILE), BF16),
                pltpu.VMEM((5, TILE, TILE), F32),
                pltpu.VMEM((5, TILE, TILE), F32),
                pltpu.SemaphoreType.DMA((SEMAPHORES,)),
                pltpu.SemaphoreType.DMA((SEMAPHORES,)),
                pltpu.SemaphoreType.DMA((2,)),
                pltpu.SemaphoreType.REGULAR,
            ],
            compiler_params=pltpu.CompilerParams(
                collective_id=0, has_side_effects=True, vmem_limit_bytes=40 << 20
            ),
        )(blocks, mask)
        return result.reshape(density.shape)

    return jax.shard_map(
        local,
        mesh=mesh,
        in_specs=(P(("row", "col"), None, None, None), P(("row", "col"), None)),
        out_specs=P(("row", "col"), None, None, None),
        check_vma=False,
    )
```

```python
import functools

import jax
import jax.numpy as jnp
from jax import lax
from jax.experimental import pallas as pl
from jax.experimental.pallas import tpu as pltpu
from jax.sharding import PartitionSpec as P

MESH = pl.DeviceIdType.MESH
F32, BF16 = jnp.float32, jnp.bfloat16
BLK = 128
K = 9
SLOTS = 2 * K
TILE = 2 * BLK

FAR = ((0, 8, 1), (1, 7, 2)), ((0, 6, 2), (1, 5, 2)), ((0, 5, 1), (1, 4, 1)), ((0, 4, 1), (1, 3, 1))
NEAR = (*FAR, ((0, 2, 2), (1, 1, 2)))

PIECES = 10


def kernel(rows, cols, x_ref, mask_ref, out_ref, held, masks, marks, high, low, s_high, s_low, square, cube, send, mask_sem, near_sem, far_sem, local_sem, ready):
    core = lax.rem(lax.axis_index("col"), 2)
    g = lax.axis_index("row") * cols + lax.axis_index("col")

    def device(index):
        index = lax.rem(index + rows * cols, rows * cols)
        return lax.div(index, cols), lax.rem(index, cols)

    slow, fast = device(g + 2 * core - 1), device(g + 1 - 2 * core)

    first, last_one = g == 0, g == rows * cols - 1
    barrier = pltpu.get_barrier_semaphore()

    @pl.when(jnp.logical_not(last_one))
    def _():
        pl.semaphore_signal(barrier, inc=1, device_id=slow, device_id_type=MESH)

    @pl.when(core == 1)
    def _():
        pl.semaphore_signal(barrier, inc=1, device_id=fast, device_id_type=MESH)

    own = pltpu.make_async_copy(x_ref, held.at[2], local_sem.at[0])
    own_mask = pltpu.make_async_copy(mask_ref, masks.at[2], local_sem.at[1])
    own.start()
    own_mask.start()

    def entry(flip, row, d):
        s = row * K + d
        return jnp.where(flip == 0, s, SLOTS - 1 - s)

    def span(flip, piece):
        row, d, count = piece
        s = row * K + d
        return pl.ds(jnp.where(flip == 0, s, SLOTS - s - count), count)

    def half(flip, r):
        return pl.ds(pl.multiple_of(jnp.where(flip == 0, r, 1 - r) * BLK, BLK), BLK)

    def place(flip, row, d):
        e = d + row
        return e // 2 - 2, half(flip, row), half(flip, e % 2)

    def start(source, target, receiving, sending, to):
        copy = pltpu.make_async_remote_copy(
            src_ref=source,
            dst_ref=target,
            send_sem=send.at[sending],
            recv_sem=receiving,
            device_id=to,
            device_id_type=MESH,
        )
        copy.start()

    def landed(target, receiving):
        pltpu.make_async_remote_copy(
            src_ref=target,
            dst_ref=target,
            send_sem=send.at[0],
            recv_sem=receiving,
            device_id=slow,
            device_id_type=MESH,
        ).wait_recv()

    def sent(source, sending):
        pltpu.make_async_remote_copy(
            src_ref=source,
            dst_ref=source,
            send_sem=send.at[sending],
            recv_sem=near_sem.at[0],
            device_id=slow,
            device_id_type=MESH,
        ).wait_send()

    def give(source, at, flip, pieces, semaphores, number, sending, to):
        for i, piece in enumerate(pieces):
            part = span(flip, piece)
            start(source.at[part], held.at[at, part], semaphores.at[number + i], sending, to)

    def take(at, flip, pieces, semaphores, number):
        for i, piece in enumerate(pieces):
            landed(held.at[at, span(flip, piece)], semaphores.at[number + i])

    def give_own(side, to):
        at, flip = 1 + 2 * side, core if side else 1 - core
        start(mask_ref, masks.at[at], mask_sem.at[side], side, to)
        for i, pieces in enumerate(NEAR):
            give(x_ref, at, flip, pieces, near_sem, PIECES * side + 2 * i, 2 + side, to)

    pl.semaphore_wait(barrier, jnp.where(first, 1, 2 - core))

    @pl.when(core == 0)
    def _():
        pl.semaphore_signal(ready, inc=1, device_id=fast, device_id_type=MESH)

    @pl.when(last_one)
    def _():
        pl.semaphore_signal(ready, inc=1, device_id=slow, device_id_type=MESH)

    @pl.when(jnp.logical_not(first))
    def _():
        give_own(0, slow)

    @pl.when(core == 1)
    def _():
        pl.semaphore_wait(ready, 1)

    give_own(1, fast)

    @pl.when(first)
    def _():
        pl.semaphore_wait(ready, 1)
        give_own(0, slow)

    for j in range(3):
        for row, d, at, k in ((0, K, j, j + 2), (1, -1, j + 2, j)):
            _, r, c = place(core, row, d)
            high[at, k, r, c] = jnp.zeros((BLK, BLK), BF16)
            low[at, k, r, c] = jnp.zeros((BLK, BLK), BF16)
    cube[...] = jnp.zeros_like(cube)

    def mark(at):
        value = masks[at].astype(F32)
        for s in range(SLOTS):
            one = value[s // K : s // K + 1, s % K : s % K + 1]
            marks[at, s : s + 1, :] = jnp.broadcast_to(one, (1, BLK))

    def split(at, flip, pieces, turned=None):
        for row, first, count in pieces:
            def one(d, carry, row=row):
                s = entry(flip, row, d)
                k, r, c = place(flip, row, d)
                value = held[at, s] * marks[at, pl.ds(s, 1), :]
                top = value.astype(BF16)
                k = at + k if turned is None else turned(k)
                high[at, k, r, c] = top
                low[at, k, r, c] = (value - top.astype(F32)).astype(BF16)
                return carry

            lax.fori_loop(first, first + count, one, 0)

    dot = functools.partial(jnp.dot, preferred_element_type=F32)

    def product(a_high, a_low, b_high, b_low):
        return dot(a_high, b_high) + (dot(a_high, b_low) + dot(a_low, b_high))

    def square_row(j, tiles, fresh=False):
        for k in tiles:
            term = product(high[2, j], low[2, j], high[j, k], low[j, k])
            square[k] = term if fresh else square[k] + term

    def cube_row(j, tiles):
        for k in tiles:
            cube[k] = cube[k] + product(s_high[j], s_low[j], high[j, k], low[j, k])

    def finish_square(j, r=slice(None), c=slice(None)):
        value = square[j, r, c]
        top = value.astype(BF16)
        s_high[j, r, c] = top
        s_low[j, r, c] = (value - top.astype(F32)).astype(BF16)

    def give_out(flip, pieces, tile):
        for row, first, count in pieces:
            def one(d, carry, row=row):
                s = entry(flip, row, d)
                k, r, c = place(flip, row, d)
                k = tile(k + 2)
                value = 3.0 * square[k, r, c] - 2.0 * cube[k, r, c]
                out_ref[s] = value * marks[2, pl.ds(s, 1), :]
                return carry

            lax.fori_loop(first, first + count, one, 0)

    own.wait()
    own_mask.wait()
    mark(2)
    split(2, core, ((0, 0, K), (1, 0, K)))

    square_row(2, range(5), fresh=True)

    for side in (1, 0):
        at, far = (3, 0) if side else (1, 4)
        flip = 1 - core if side else core
        other = slow if side else fast
        landed(masks.at[at], mask_sem.at[side])
        start(masks.at[at], masks.at[far], mask_sem.at[3 - side], 4 + side, other)
        mark(at)
        for i, pieces in enumerate(NEAR):
            take(at, flip, pieces, near_sem, PIECES * side + 2 * i)
            if i < len(FAR):
                give(held.at[at], far, flip, pieces, far_sem, PIECES * (1 - side) + 2 * i, 6 + side, other)
            split(at, flip, pieces, turned=(lambda k: 3 - k) if side else None)
            if i != 2:
                k = (3, 2, 1, 1, 0)[i]
                square_row(at, (4 - k if side else k,))

    for last in (False, True):
        side = jnp.where((g == 1) == last, 1, 0)
        flip = jnp.where(side == 0, core, 1 - core)

        def tile(k, side=side):
            return jnp.where(side == 0, k, 4 - k)

        far = tile(0)
        landed(masks.at[far], mask_sem.at[2 + side])
        mark(far)
        for i, pieces in enumerate(FAR):
            take(far, flip, pieces, far_sem, PIECES * side + 2 * i)
            split(far, flip, pieces, turned=lambda k: tile(k))
            if i == 0:
                square_row(far, (2,))
                if last:
                    finish_square(2)
                    cube_row(2, range(5))
            elif i == 1:
                square_row(far, (tile(1),))
                finish_square(tile(1))
                cube_row(tile(1), [tile(k) for k in range(4)])
            elif i == 2:
                r0, r1 = half(flip, 0), half(flip, 1)
                c0, c1 = r0, r1
                everything = slice(None)
                square[far, :, c1] += product(high[2, far], low[2, far], high[far, far, :, c1], low[far, far, :, c1])
                finish_square(far, everything, c1)
                a_high, a_low = s_high[far, :, c1], s_low[far, :, c1]
                for k in (tile(1), tile(2)):
                    cube[k] += product(a_high, a_low, high[far, k, c1, :], low[far, k, c1, :])
                cube[far, :, c1] += product(a_high, a_low, high[far, far, c1, c1], low[far, far, c1, c1])
                if last:
                    give_out(flip, ((0, 5, 4), (1, 0, K)), tile)
            else:
                square[far, r0, c0] += product(high[2, far, r0, :], low[2, far, r0, :], high[far, far, :, c0], low[far, far, :, c0])
                finish_square(far, r0, c0)
                a_high, a_low = s_high[far, r0, c0], s_low[far, r0, c0]
                cube[far, r0, c0] += product(s_high[far, r0, :], s_low[far, r0, :], high[far, far, :, c0], low[far, far, :, c0])
                cube[far, r0, c1] += product(a_high, a_low, high[far, far, c0, c1], low[far, far, c0, c1])
                k = tile(1)
                cube[k, r0, :] += product(a_high, a_low, high[far, k, c0, :], low[far, k, c0, :])
                cube[2, r0, c0] += product(a_high, a_low, high[far, 2, c0, c0], low[far, 2, c0, c0])
                if last:
                    give_out(flip, ((0, 0, 5),), tile)

    for n in range(2):
        sent(masks.at[2], n)
        sent(held.at[2, pl.ds(0, 15)], 2 + n)
        sent(masks.at[2], 4 + n)
        sent(held.at[2, pl.ds(0, 11)], 6 + n)


def solution(mesh):
    rows, cols = mesh.shape["row"], mesh.shape["col"]

    def local(density, band_mask):
        blocks = pltpu.with_memory_space_constraint(
            density.reshape(SLOTS, BLK, BLK), pltpu.HBM
        )
        mask = pltpu.with_memory_space_constraint(band_mask, pltpu.HBM)
        result = pl.pallas_call(
            functools.partial(kernel, rows, cols),
            out_shape=jax.ShapeDtypeStruct((SLOTS, BLK, BLK), F32),
            in_specs=[
                pl.BlockSpec(memory_space=pltpu.HBM),
                pl.BlockSpec(memory_space=pltpu.HBM),
            ],
            out_specs=pl.BlockSpec(memory_space=pltpu.VMEM),
            scratch_shapes=[
                pltpu.VMEM((5, SLOTS, BLK, BLK), F32),
                pltpu.VMEM((5, 2, K), jnp.int32),
                pltpu.VMEM((5, 24, BLK), F32),
                pltpu.VMEM((5, 5, TILE, TILE), BF16),
                pltpu.VMEM((5, 5, TILE, TILE), BF16),
                pltpu.VMEM((5, TILE, TILE), BF16),
                pltpu.VMEM((5, TILE, TILE), BF16),
                pltpu.VMEM((5, TILE, TILE), F32),
                pltpu.VMEM((5, TILE, TILE), F32),
                pltpu.SemaphoreType.DMA((8,)),
                pltpu.SemaphoreType.DMA((4,)),
                pltpu.SemaphoreType.DMA((2 * PIECES,)),
                pltpu.SemaphoreType.DMA((2 * PIECES,)),
                pltpu.SemaphoreType.DMA((2,)),
                pltpu.SemaphoreType.REGULAR,
            ],
            compiler_params=pltpu.CompilerParams(
                collective_id=0, has_side_effects=True, vmem_limit_bytes=40 << 20
            ),
        )(blocks, mask)
        return result.reshape(density.shape)

    return jax.shard_map(
        local,
        mesh=mesh,
        in_specs=(P(("row", "col"), None, None, None), P(("row", "col"), None)),
        out_specs=P(("row", "col"), None, None, None),
        check_vma=False,
    )
```

```python
import functools

import jax
import jax.numpy as jnp
from jax import lax
from jax.experimental import pallas as pl
from jax.experimental.pallas import tpu as pltpu
from jax.sharding import PartitionSpec as P

MESH = pl.DeviceIdType.MESH
F32, BF16 = jnp.float32, jnp.bfloat16
BLK = 128
K = 9
SLOTS = 2 * K
TILE = 2 * BLK

FAR = ((0, 8, 1), (1, 7, 2)), ((0, 6, 2), (1, 5, 2)), ((0, 5, 1), (1, 4, 1)), ((0, 4, 1), (1, 3, 1))
NEAR = (*FAR, ((0, 2, 2), (1, 1, 2)))

PIECES = 10


def kernel(rows, cols, x_ref, mask_ref, out_ref, held, masks, marks, high, low, s_high, s_low, square, cube, send, mask_sem, near_sem, far_sem, local_sem, ready):
    mine, col = lax.axis_index("row"), lax.axis_index("col")
    core, g = lax.rem(col, 2), mine * cols + col

    def device(index):
        index = lax.rem(index + rows * cols, rows * cols)
        return lax.div(index, cols), lax.rem(index, cols)

    slow, fast = device(g + 2 * core - 1), device(g + 1 - 2 * core)

    first, second, last = g == 0, g == 1, g == rows * cols - 1
    barrier = pltpu.get_barrier_semaphore()

    def here(condition, *others):
        @pl.when(condition)
        def _():
            for other in others:
                pl.semaphore_signal(barrier, inc=1, device_id=other, device_id_type=MESH)

    here(jnp.logical_not(last), slow)
    here(core == 1, fast)
    here(second, (rows - 1, cols - 1))

    own = pltpu.make_async_copy(x_ref, held.at[2], local_sem.at[0])
    own_mask = pltpu.make_async_copy(mask_ref, masks.at[2], local_sem.at[1])
    own.start()
    own_mask.start()

    def entry(flip, row, d):
        s = row * K + d
        return jnp.where(flip == 0, s, SLOTS - 1 - s)

    def span(flip, piece):
        row, d, count = piece
        s = row * K + d
        return pl.ds(jnp.where(flip == 0, s, SLOTS - s - count), count)

    def half(flip, r):
        return pl.ds(pl.multiple_of(jnp.where(flip == 0, r, 1 - r) * BLK, BLK), BLK)

    def place(flip, row, d):
        e = d + row
        return e // 2 - 2, half(flip, row), half(flip, e % 2)

    def start(source, target, receiving, sending, to):
        copy = pltpu.make_async_remote_copy(
            src_ref=source,
            dst_ref=target,
            send_sem=send.at[sending],
            recv_sem=receiving,
            device_id=to,
            device_id_type=MESH,
        )
        copy.start()

    def landed(target, receiving):
        pltpu.make_async_remote_copy(
            src_ref=target,
            dst_ref=target,
            send_sem=send.at[0],
            recv_sem=receiving,
            device_id=slow,
            device_id_type=MESH,
        ).wait_recv()

    def sent(source, sending):
        pltpu.make_async_remote_copy(
            src_ref=source,
            dst_ref=source,
            send_sem=send.at[sending],
            recv_sem=near_sem.at[0],
            device_id=slow,
            device_id_type=MESH,
        ).wait_send()

    def give(source, at, flip, pieces, semaphores, number, sending, to):
        for i, piece in enumerate(pieces):
            part = span(flip, piece)
            start(source.at[part], held.at[at, part], semaphores.at[number + i], sending, to)

    def take(at, flip, pieces, semaphores, number):
        for i, piece in enumerate(pieces):
            landed(held.at[at, span(flip, piece)], semaphores.at[number + i])

    def give_mask(at, semaphore, side, to):
        start(mask_ref, masks.at[at], mask_sem.at[semaphore], side, to)

    pl.semaphore_wait(barrier, jnp.where(first, 1, jnp.where(last, 2, 2 - core)))

    @pl.when(core == 0)
    def _():
        pl.semaphore_signal(ready, inc=1, device_id=fast, device_id_type=MESH)

    @pl.when(last)
    def _():
        pl.semaphore_signal(ready, inc=1, device_id=slow, device_id_type=MESH)

    def give_slow():
        give_mask(1, 0, 0, slow)
        for i, pieces in enumerate(FAR):
            give(x_ref, 1, 1 - core, pieces, near_sem, 2 * i, 2, slow)
        give_rest()

    def give_rest():
        give(x_ref, 1, 1 - core, NEAR[4], near_sem, 8, 2, slow)

    @pl.when(jnp.logical_not(jnp.logical_or(first, last)))
    def _():
        give_slow()

    @pl.when(last)
    def _():
        give_mask(4, 3, 0, (0, 1))
        for i, pieces in enumerate(FAR):
            give(x_ref, 4, 0, pieces, far_sem, PIECES + 2 * i, 2, (0, 1))
        give_rest()

    @pl.when(core == 1)
    def _():
        pl.semaphore_wait(ready, 1)

    give_mask(3, 1, 1, fast)
    for i, pieces in enumerate(NEAR):
        give(x_ref, 3, core, pieces, near_sem, PIECES + 2 * i, 3, fast)

    @pl.when(first)
    def _():
        pl.semaphore_wait(ready, 1)
        give_slow()

    for j in range(3):
        for row, d, at, k in ((0, K, j, j + 2), (1, -1, j + 2, j)):
            _, r, c = place(core, row, d)
            high[at, k, r, c] = jnp.zeros((BLK, BLK), BF16)
            low[at, k, r, c] = jnp.zeros((BLK, BLK), BF16)
    cube[...] = jnp.zeros_like(cube)

    def mark(at):
        value = masks[at].astype(F32)
        for s in range(SLOTS):
            one = value[s // K : s // K + 1, s % K : s % K + 1]
            marks[at, s : s + 1, :] = jnp.broadcast_to(one, (1, BLK))

    def split(at, flip, pieces, turned=None):
        for row, first, count in pieces:
            def one(d, carry, row=row):
                s = entry(flip, row, d)
                k, r, c = place(flip, row, d)
                value = held[at, s] * marks[at, pl.ds(s, 1), :]
                top = value.astype(BF16)
                k = at + k if turned is None else turned(k)
                high[at, k, r, c] = top
                low[at, k, r, c] = (value - top.astype(F32)).astype(BF16)
                return carry

            lax.fori_loop(first, first + count, one, 0, unroll=count < 3)

    dot = functools.partial(jnp.dot, preferred_element_type=F32)

    def product(a_high, a_low, b_high, b_low):
        return dot(a_high, b_high) + (dot(a_high, b_low) + dot(a_low, b_high))

    def square_row(j, tiles, fresh=False):
        for k in tiles:
            term = product(high[2, j], low[2, j], high[j, k], low[j, k])
            square[k] = term if fresh else square[k] + term

    def cube_row(j, tiles):
        for k in tiles:
            cube[k] = cube[k] + product(s_high[j], s_low[j], high[j, k], low[j, k])

    def finish_square(j, r=slice(None), c=slice(None)):
        value = square[j, r, c]
        top = value.astype(BF16)
        s_high[j, r, c] = top
        s_low[j, r, c] = (value - top.astype(F32)).astype(BF16)

    def give_out(flip, pieces, tile):
        for row, first, count in pieces:
            def one(d, carry, row=row):
                s = entry(flip, row, d)
                k, r, c = place(flip, row, d)
                k = tile(k + 2)
                value = 3.0 * square[k, r, c] - 2.0 * cube[k, r, c]
                out_ref[s] = value * marks[2, pl.ds(s, 1), :]
                return carry

            lax.fori_loop(first, first + count, one, 0, unroll=True)

    own.wait()
    own_mask.wait()
    mark(2)
    split(2, core, ((0, 0, K), (1, 0, K)))

    square_row(2, range(5), fresh=True)

    def pass_on(side, i=None):
        at, far, flip, other = (3, 0, 1 - core, slow) if side else (1, 4, core, fast)
        if i is None:
            start(masks.at[at], masks.at[far], mask_sem.at[3 - side], 4 + side, other)
        else:
            give(held.at[at], far, flip, FAR[i], far_sem, PIECES * (1 - side) + 2 * i, 6 + side, other)

    def near(side, i):
        at, flip = (3, 1 - core) if side else (1, core)
        take(at, flip, NEAR[i], near_sem, PIECES * side + 2 * i)
        if i < 4 and side:
            pass_on(side, i)
        elif i < 4:
            pl.when(jnp.logical_not(first))(lambda: pass_on(side, i))
        split(at, flip, NEAR[i], turned=(lambda k: 3 - k) if side else None)
        if i != 2:
            k = (3, 2, 1, 1, 0)[i]
            square_row(at, (4 - k if side else k,))

    for side in (1, 0):
        at = 3 if side else 1
        landed(masks.at[at], mask_sem.at[side])
        if side:
            pass_on(side)
        else:
            pl.when(jnp.logical_not(first))(lambda: pass_on(0))
        mark(at)
        for i in range(5):
            near(side, i)

    for final in (False, True):
        side = jnp.where(second == final, 1, 0)
        flip = jnp.where(side == 0, core, 1 - core)

        def tile(k, side=side):
            return jnp.where(side == 0, k, 4 - k)

        far = tile(0)
        landed(masks.at[far], mask_sem.at[2 + side])
        if final:
            pl.when(second)(lambda: start(masks.at[4], masks.at[1], mask_sem.at[0], 8, fast))
        mark(far)
        for i, pieces in enumerate(FAR):
            take(far, flip, pieces, far_sem, PIECES * side + 2 * i)
            if final:
                pl.when(second)(lambda: give(held.at[4], 1, 0, pieces, near_sem, 2 * i, 9, fast))
            split(far, flip, pieces, turned=lambda k: tile(k))
            if i == 0:
                square_row(far, (2,))
                if final:
                    finish_square(2)
                    cube_row(2, range(5))
            elif i == 1:
                square_row(far, (tile(1),))
                finish_square(tile(1))
                cube_row(tile(1), [tile(k) for k in range(4)])
            elif i == 2:
                r0, r1 = half(flip, 0), half(flip, 1)
                c0, c1 = r0, r1
                everything = slice(None)
                square[far, :, c1] += product(high[2, far], low[2, far], high[far, far, :, c1], low[far, far, :, c1])
                finish_square(far, everything, c1)
                a_high, a_low = s_high[far, :, c1], s_low[far, :, c1]
                for k in (tile(1), tile(2)):
                    cube[k] += product(a_high, a_low, high[far, k, c1, :], low[far, k, c1, :])
                cube[far, :, c1] += product(a_high, a_low, high[far, far, c1, c1], low[far, far, c1, c1])
                if final:
                    give_out(flip, ((0, 5, 4), (1, 0, K)), tile)
            else:
                square[far, r0, c0] += product(high[2, far, r0, :], low[2, far, r0, :], high[far, far, :, c0], low[far, far, :, c0])
                finish_square(far, r0, c0)
                a_high, a_low = s_high[far, r0, c0], s_low[far, r0, c0]
                cube[far, r0, c0] += product(s_high[far, r0, :], s_low[far, r0, :], high[far, far, :, c0], low[far, far, :, c0])
                cube[far, r0, c1] += product(a_high, a_low, high[far, far, c0, c1], low[far, far, c0, c1])
                k = tile(1)
                cube[k, r0, :] += product(a_high, a_low, high[far, k, c0, :], low[far, k, c0, :])
                cube[2, r0, c0] += product(a_high, a_low, high[far, 2, c0, c0], low[far, 2, c0, c0])
                if final:
                    give_out(flip, ((0, 0, 5),), tile)

    def all_sent(first_sem, count):
        sent(masks.at[2], first_sem)
        sent(held.at[2, pl.ds(0, count)], first_sem + 1 if first_sem > 7 else first_sem + 2)

    all_sent(0, 15)
    all_sent(1, 15)
    all_sent(5, 11)
    pl.when(jnp.logical_not(first))(lambda: all_sent(4, 11))
    pl.when(second)(lambda: all_sent(8, 11))


def solution(mesh):
    rows, cols = mesh.shape["row"], mesh.shape["col"]

    def local(density, band_mask):
        blocks = pltpu.with_memory_space_constraint(
            density.reshape(SLOTS, BLK, BLK), pltpu.HBM
        )
        mask = pltpu.with_memory_space_constraint(band_mask, pltpu.HBM)
        result = pl.pallas_call(
            functools.partial(kernel, rows, cols),
            out_shape=jax.ShapeDtypeStruct((SLOTS, BLK, BLK), F32),
            in_specs=[
                pl.BlockSpec(memory_space=pltpu.HBM),
                pl.BlockSpec(memory_space=pltpu.HBM),
            ],
            out_specs=pl.BlockSpec(memory_space=pltpu.VMEM),
            scratch_shapes=[
                pltpu.VMEM((5, SLOTS, BLK, BLK), F32),
                pltpu.VMEM((5, 2, K), jnp.int32),
                pltpu.VMEM((5, 24, BLK), F32),
                pltpu.VMEM((5, 5, TILE, TILE), BF16),
                pltpu.VMEM((5, 5, TILE, TILE), BF16),
                pltpu.VMEM((5, TILE, TILE), BF16),
                pltpu.VMEM((5, TILE, TILE), BF16),
                pltpu.VMEM((5, TILE, TILE), F32),
                pltpu.VMEM((5, TILE, TILE), F32),
                pltpu.SemaphoreType.DMA((10,)),
                pltpu.SemaphoreType.DMA((4,)),
                pltpu.SemaphoreType.DMA((2 * PIECES,)),
                pltpu.SemaphoreType.DMA((2 * PIECES,)),
                pltpu.SemaphoreType.DMA((2,)),
                pltpu.SemaphoreType.REGULAR,
            ],
            compiler_params=pltpu.CompilerParams(
                collective_id=0, has_side_effects=True, vmem_limit_bytes=40 << 20
            ),
        )(blocks, mask)
        return result.reshape(density.shape)

    return jax.shard_map(
        local,
        mesh=mesh,
        in_specs=(P(("row", "col"), None, None, None), P(("row", "col"), None)),
        out_specs=P(("row", "col"), None, None, None),
        check_vma=False,
    )
```

```python
import functools

import jax
import jax.numpy as jnp
from jax import lax
from jax.experimental import pallas as pl
from jax.experimental.pallas import tpu as pltpu
from jax.sharding import PartitionSpec as P

MESH = pl.DeviceIdType.MESH
F32, BF16 = jnp.float32, jnp.bfloat16
BLK = 128
K = 9
SLOTS = 2 * K
TILE = 2 * BLK

FAR = ((0, 8, 1), (1, 7, 2)), ((0, 6, 2), (1, 5, 2)), ((0, 5, 1), (1, 4, 1)), ((0, 4, 1), (1, 3, 1))
NEAR = (*FAR, ((0, 2, 2), (1, 1, 2)))

PIECES = 10


def entry(flip, row, d):
    s = row * K + d
    return jnp.where(flip == 0, s, SLOTS - 1 - s)


def span(flip, piece):
    row, d, count = piece
    s = row * K + d
    return pl.ds(jnp.where(flip == 0, s, SLOTS - s - count), count)


def half(flip, r):
    return pl.ds(pl.multiple_of(jnp.where(flip == 0, r, 1 - r) * BLK, BLK), BLK)


def product(a_high, a_low, b_high, b_low):
    dot = functools.partial(jnp.dot, preferred_element_type=F32)
    return dot(a_high, b_high) + (dot(a_high, b_low) + dot(a_low, b_high))


def kernel(rows, cols, x_ref, mask_ref, out_ref, marks, high, low, s_high, s_low, square, cube, held, masks, send, mask_sem, near_sem, far_sem, local_sem, ready):
    mine, col = lax.axis_index("row"), lax.axis_index("col")
    core, g = lax.rem(col, 2), mine * cols + col

    def device(index):
        index = lax.rem(index + rows * cols, rows * cols)
        return lax.div(index, cols), lax.rem(index, cols)

    slow, fast = device(g + 2 * core - 1), device(g + 1 - 2 * core)

    first, second, last = g == 0, g == 1, g == rows * cols - 1
    barrier = pltpu.get_barrier_semaphore()

    def here(condition, *others):
        @pl.when(condition)
        def _():
            for other in others:
                pl.semaphore_signal(barrier, inc=1, device_id=other, device_id_type=MESH)

    here(jnp.logical_not(last), slow)
    here(core == 1, fast)
    here(second, (rows - 1, cols - 1))

    own = pltpu.make_async_copy(x_ref, held.at[2], local_sem.at[0])
    own_mask = pltpu.make_async_copy(mask_ref, masks.at[2], local_sem.at[1])

    def place(flip, row, d):
        e = d + row
        return e // 2 - 2, half(flip, row), half(flip, e % 2)

    def start(source, target, receiving, sending, to):
        copy = pltpu.make_async_remote_copy(
            src_ref=source,
            dst_ref=target,
            send_sem=send.at[sending],
            recv_sem=receiving,
            device_id=to,
            device_id_type=MESH,
        )
        copy.start()

    def landed(target, receiving):
        pltpu.make_async_remote_copy(
            src_ref=target,
            dst_ref=target,
            send_sem=send.at[0],
            recv_sem=receiving,
            device_id=slow,
            device_id_type=MESH,
        ).wait_recv()

    def sent(source, sending):
        pltpu.make_async_remote_copy(
            src_ref=source,
            dst_ref=source,
            send_sem=send.at[sending],
            recv_sem=near_sem.at[0],
            device_id=slow,
            device_id_type=MESH,
        ).wait_send()

    def give(source, at, flip, pieces, semaphores, number, sending, to):
        for i, piece in enumerate(pieces):
            part = span(flip, piece)
            start(source.at[part], held.at[at, part], semaphores.at[number + i], sending, to)

    def take(at, flip, pieces, semaphores, number):
        for i, piece in enumerate(pieces):
            landed(held.at[at, span(flip, piece)], semaphores.at[number + i])

    def give_mask(at, semaphore, side, to):
        start(mask_ref, masks.at[at], mask_sem.at[semaphore], side, to)

    pl.semaphore_wait(barrier, jnp.where(first, 1, jnp.where(last, 2, 2 - core)))

    @pl.when(core == 0)
    def _():
        pl.semaphore_signal(ready, inc=1, device_id=fast, device_id_type=MESH)

    @pl.when(last)
    def _():
        pl.semaphore_signal(ready, inc=1, device_id=slow, device_id_type=MESH)

    def give_slow():
        give_mask(1, 0, 0, slow)
        for i, pieces in enumerate(FAR):
            give(x_ref, 1, 1 - core, pieces, near_sem, 2 * i, 2, slow)
        give_rest()

    def give_rest():
        give(x_ref, 1, 1 - core, NEAR[4], near_sem, 8, 2, slow)

    @pl.when(jnp.logical_not(jnp.logical_or(first, last)))
    def _():
        give_slow()

    @pl.when(last)
    def _():
        give_mask(4, 3, 0, (0, 1))
        for i, pieces in enumerate(FAR):
            give(x_ref, 4, 0, pieces, far_sem, PIECES + 2 * i, 2, (0, 1))
        give_rest()

    own.start()
    own_mask.start()

    @pl.when(core == 1)
    def _():
        pl.semaphore_wait(ready, 1)

    give_mask(3, 1, 1, fast)
    for i, pieces in enumerate(NEAR):
        give(x_ref, 3, core, pieces, near_sem, PIECES + 2 * i, 3, fast)

    @pl.when(first)
    def _():
        pl.semaphore_wait(ready, 1)
        give_slow()

    for j in range(3):
        for row, d, at, k in ((0, K, j, j + 2), (1, -1, j + 2, j)):
            _, r, c = place(core, row, d)
            high[at, k, r, c] = jnp.zeros((BLK, BLK), BF16)
            low[at, k, r, c] = jnp.zeros((BLK, BLK), BF16)
    cube[...] = jnp.zeros_like(cube)

    def mark(at):
        value = masks[at].astype(F32)
        for s in range(SLOTS):
            one = value[s // K : s // K + 1, s % K : s % K + 1]
            marks[at, s : s + 1, :] = jnp.broadcast_to(one, (1, BLK))

    def split(at, flip, pieces, turned=None):
        for row, first, count in pieces:
            def one(d, carry, row=row):
                s = entry(flip, row, d)
                k, r, c = place(flip, row, d)
                value = held[at, s] * marks[at, pl.ds(s, 1), :]
                top = value.astype(BF16)
                k = at + k if turned is None else turned(k)
                high[at, k, r, c] = top
                low[at, k, r, c] = (value - top.astype(F32)).astype(BF16)
                return carry

            if count < 3:
                for d in range(first, first + count):
                    one(d, 0)
            else:
                lax.fori_loop(first, first + count, one, 0)

    def square_row(j, tiles, fresh=False):
        for k in tiles:
            term = product(high[2, j], low[2, j], high[j, k], low[j, k])
            square[k] = term if fresh else square[k] + term

    def cube_row(j, tiles):
        for k in tiles:
            cube[k] = cube[k] + product(s_high[j], s_low[j], high[j, k], low[j, k])

    def finish_square(j, r=slice(None), c=slice(None)):
        value = square[j, r, c]
        top = value.astype(BF16)
        s_high[j, r, c] = top
        s_low[j, r, c] = (value - top.astype(F32)).astype(BF16)

    def give_out(flip, pieces, tile):
        for row, first, count in pieces:
            def one(d, carry, row=row):
                s = entry(flip, row, d)
                k, r, c = place(flip, row, d)
                k = tile(k + 2)
                value = 3.0 * square[k, r, c] - 2.0 * cube[k, r, c]
                out_ref[s] = value * marks[2, pl.ds(s, 1), :]
                return carry

            for d in range(first, first + count):
                one(d, 0)

    own.wait()
    own_mask.wait()
    mark(2)
    split(2, core, ((0, 0, K), (1, 0, K)))

    square_row(2, range(5), fresh=True)

    def pass_on(side, i=None):
        at, far, flip, other = (3, 0, 1 - core, slow) if side else (1, 4, core, fast)
        if i is None:
            start(masks.at[at], masks.at[far], mask_sem.at[3 - side], 4 + side, other)
        else:
            give(held.at[at], far, flip, FAR[i], far_sem, PIECES * (1 - side) + 2 * i, 6 + side, other)

    def near(side, i):
        at, flip = (3, 1 - core) if side else (1, core)
        take(at, flip, NEAR[i], near_sem, PIECES * side + 2 * i)
        if i < 4 and side:
            pass_on(side, i)
        elif i < 4:
            pl.when(jnp.logical_not(first))(lambda: pass_on(side, i))
        split(at, flip, NEAR[i], turned=(lambda k: 3 - k) if side else None)
        if i != 2:
            k = (3, 2, 1, 1, 0)[i]
            square_row(at, (4 - k if side else k,))

    for side in (1, 0):
        at = 3 if side else 1
        landed(masks.at[at], mask_sem.at[side])
        if side:
            pass_on(side)
        else:
            pl.when(jnp.logical_not(first))(lambda: pass_on(0))
        mark(at)
        for i in range(5):
            near(side, i)

    for final in (False, True):
        side = jnp.where(second == final, 1, 0)
        flip = jnp.where(side == 0, core, 1 - core)

        def tile(k, side=side):
            return jnp.where(side == 0, k, 4 - k)

        far = tile(0)
        landed(masks.at[far], mask_sem.at[2 + side])
        if final:
            pl.when(second)(lambda: start(masks.at[4], masks.at[1], mask_sem.at[0], 8, fast))
        mark(far)
        for i, pieces in enumerate(FAR):
            take(far, flip, pieces, far_sem, PIECES * side + 2 * i)
            if final:
                pl.when(second)(lambda: give(held.at[4], 1, 0, pieces, near_sem, 2 * i, 9, fast))
            split(far, flip, pieces, turned=lambda k: tile(k))
            if i == 0:
                square_row(far, (2,))
                if final:
                    finish_square(2)
                    cube_row(2, range(5))
            elif i == 1:
                square_row(far, (tile(1),))
                finish_square(tile(1))
                cube_row(tile(1), [tile(k) for k in range(4)])
            elif i == 2:
                r0, r1 = half(flip, 0), half(flip, 1)
                c0, c1 = r0, r1
                everything = slice(None)
                square[far, :, c1] += product(high[2, far], low[2, far], high[far, far, :, c1], low[far, far, :, c1])
                finish_square(far, everything, c1)
                a_high, a_low = s_high[far, :, c1], s_low[far, :, c1]
                for k in (tile(1), tile(2)):
                    cube[k] += product(a_high, a_low, high[far, k, c1, :], low[far, k, c1, :])
                cube[far, :, c1] += product(a_high, a_low, high[far, far, c1, c1], low[far, far, c1, c1])
                if final:
                    give_out(flip, ((0, 5, 4), (1, 0, K)), tile)
            elif not final:
                square[far, r0, c0] += product(high[2, far, r0, :], low[2, far, r0, :], high[far, far, :, c0], low[far, far, :, c0])
                finish_square(far, r0, c0)
                a_high, a_low = s_high[far, r0, c0], s_low[far, r0, c0]
                cube[far, r0, c0] += product(s_high[far, r0, :], s_low[far, r0, :], high[far, far, :, c0], low[far, far, :, c0])
                cube[far, r0, c1] += product(a_high, a_low, high[far, far, c0, c1], low[far, far, c0, c1])
                k = tile(1)
                cube[k, r0, :] += product(a_high, a_low, high[far, k, c0, :], low[far, k, c0, :])
                cube[2, r0, c0] += product(a_high, a_low, high[far, 2, c0, c0], low[far, 2, c0, c0])

    def all_sent(first_sem, count):
        sent(masks.at[2], first_sem)
        sent(held.at[2, pl.ds(0, count)], first_sem + 1 if first_sem > 7 else first_sem + 2)

    all_sent(0, 15)
    all_sent(1, 15)
    all_sent(5, 11)
    pl.when(jnp.logical_not(first))(lambda: all_sent(4, 11))
    pl.when(second)(lambda: all_sent(8, 11))


def finish(cols, part_ref, marks, high, low, s_high, s_low, square, cube, out_ref, rest, sems):
    g = lax.axis_index("row") * cols + lax.axis_index("col")
    core, second = lax.rem(g, 2), g == 1
    flip = jnp.where(second, 1 - core, core)
    far, near = jnp.where(second, 4, 0), jnp.where(second, 3, 1)
    copies = []

    def write(source, target, n):
        copy = pltpu.make_async_copy(source, out_ref.at[target], sems.at[n])
        copy.start()
        copies.append(copy)

    for n, piece in enumerate(((1, 0, K), (0, 5, 4))):
        part = span(flip, piece)
        write(part_ref.at[part], part, n)

    r0, c0, c1 = half(flip, 0), half(flip, 0), half(flip, 1)

    def times(a, j, k, r, c):
        return product(*a, high[j, k, r, c], low[j, k, r, c])

    def put(d, at, s_block, c_block):
        mark = marks[2, pl.ds(entry(flip, 0, d), 1), :]
        rest[at] = (3.0 * s_block - 2.0 * c_block) * mark

    whole = slice(None)
    corner = square[far, r0, c0] + times((high[2, far, r0, :], low[2, far, r0, :]), far, far, whole, c0)
    top = corner.astype(BF16)
    left = top, (corner - top.astype(F32)).astype(BF16)
    beside = s_high[far, r0, c1], s_low[far, r0, c1]

    def at(d):
        return jnp.where(flip == 0, d, 4 - d)

    put(0, at(0), corner, cube[far, r0, c0] + times(left, far, far, c0, c0) + times(beside, far, far, c1, c0))
    put(1, at(1), square[far, r0, c1], cube[far, r0, c1] + times(left, far, far, c0, c1))
    both = cube[near, r0, :] + times(left, far, near, c0, whole)
    for h in range(2):
        columns = slice(h * BLK, (h + 1) * BLK)
        d = jnp.where(flip == 0, 2 + h, 3 - h)
        put(d, at(d), square[near, r0, columns], both[:, columns])
    put(4, at(4), square[2, r0, c0], cube[2, r0, c0] + times(left, far, 2, c0, c0))

    write(rest, span(flip, (0, 0, 5)), 2)
    for copy in copies:
        copy.wait()


def solution(mesh):
    rows, cols = mesh.shape["row"], mesh.shape["col"]

    def local(density, band_mask):
        blocks = pltpu.with_memory_space_constraint(
            density.reshape(SLOTS, BLK, BLK), pltpu.HBM
        )
        mask = pltpu.with_memory_space_constraint(band_mask, pltpu.HBM)
        tiles, line = (5, 5, TILE, TILE), (5, TILE, TILE)
        blocks_shape = jax.ShapeDtypeStruct((SLOTS, BLK, BLK), F32)
        vmem = pl.BlockSpec(memory_space=pltpu.VMEM)
        parts = pl.pallas_call(
            functools.partial(kernel, rows, cols),
            out_shape=[
                blocks_shape,
                jax.ShapeDtypeStruct((5, 24, BLK), F32),
                jax.ShapeDtypeStruct(tiles, BF16),
                jax.ShapeDtypeStruct(tiles, BF16),
                jax.ShapeDtypeStruct(line, BF16),
                jax.ShapeDtypeStruct(line, BF16),
                jax.ShapeDtypeStruct(line, F32),
                jax.ShapeDtypeStruct(line, F32),
            ],
            in_specs=[
                pl.BlockSpec(memory_space=pltpu.HBM),
                pl.BlockSpec(memory_space=pltpu.HBM),
            ],
            out_specs=[vmem] * 8,
            scratch_shapes=[
                pltpu.VMEM((5, SLOTS, BLK, BLK), F32),
                pltpu.VMEM((5, 2, K), jnp.int32),
                pltpu.SemaphoreType.DMA((10,)),
                pltpu.SemaphoreType.DMA((4,)),
                pltpu.SemaphoreType.DMA((2 * PIECES,)),
                pltpu.SemaphoreType.DMA((2 * PIECES,)),
                pltpu.SemaphoreType.DMA((2,)),
                pltpu.SemaphoreType.REGULAR,
            ],
            compiler_params=pltpu.CompilerParams(
                collective_id=0, has_side_effects=True, vmem_limit_bytes=24 << 20
            ),
        )(blocks, mask)
        result = pl.pallas_call(
            functools.partial(finish, cols),
            out_shape=blocks_shape,
            in_specs=[vmem] * 8,
            out_specs=pl.BlockSpec(memory_space=pltpu.HBM),
            scratch_shapes=[
                pltpu.VMEM((5, BLK, BLK), F32),
                pltpu.SemaphoreType.DMA((3,)),
            ],
            compiler_params=pltpu.CompilerParams(vmem_limit_bytes=4 << 20),
        )(*parts)
        return result.reshape(density.shape)

    return jax.shard_map(
        local,
        mesh=mesh,
        in_specs=(P(("row", "col"), None, None, None), P(("row", "col"), None)),
        out_specs=P(("row", "col"), None, None, None),
        check_vma=False,
    )
```

```python
import functools

import jax
import jax.numpy as jnp
from jax import lax
from jax.experimental import pallas as pl
from jax.experimental.pallas import tpu as pltpu
from jax.sharding import PartitionSpec as P

MESH = pl.DeviceIdType.MESH
F32, BF16 = jnp.float32, jnp.bfloat16
BLK = 128
K = 9
SLOTS = 2 * K
TILE = 2 * BLK

FAR = ((0, 8, 1), (1, 7, 2)), ((0, 6, 2), (1, 5, 2)), ((0, 5, 1), (1, 4, 1)), ((0, 4, 1), (1, 3, 1))
NEAR = (*FAR, ((0, 2, 2), (1, 1, 2)))
MOST = (0, 4, 5), (1, 3, 6)

PIECES = 10


def entry(flip, row, d):
    s = row * K + d
    return jnp.where(flip == 0, s, SLOTS - 1 - s)


def span(flip, piece):
    row, d, count = piece
    s = row * K + d
    return pl.ds(jnp.where(flip == 0, s, SLOTS - s - count), count)


def half(flip, r):
    return pl.ds(pl.multiple_of(jnp.where(flip == 0, r, 1 - r) * BLK, BLK), BLK)


def product(a_high, a_low, b_high, b_low):
    dot = functools.partial(jnp.dot, preferred_element_type=F32)
    return dot(a_high, b_high) + (dot(a_high, b_low) + dot(a_low, b_high))


def kernel(rows, cols, x_ref, mask_ref, out_ref, marks, high, low, s_high, s_low, square, cube, held, masks, send, mask_sem, near_sem, far_sem, local_sem, ready):
    mine, col = lax.axis_index("row"), lax.axis_index("col")
    core, g = lax.rem(col, 2), mine * cols + col

    def device(index):
        index = lax.rem(index + rows * cols, rows * cols)
        return lax.div(index, cols), lax.rem(index, cols)

    slow, fast = device(g + 2 * core - 1), device(g + 1 - 2 * core)

    first, second, last = g == 0, g == 1, g == rows * cols - 1
    barrier = pltpu.get_barrier_semaphore()

    def here(condition, *others):
        @pl.when(condition)
        def _():
            for other in others:
                pl.semaphore_signal(barrier, inc=1, device_id=other, device_id_type=MESH)

    here(jnp.logical_not(last), slow)
    here(core == 1, fast)
    here(second, (rows - 1, cols - 1))

    own = pltpu.make_async_copy(x_ref, held.at[2], local_sem.at[0])
    own_mask = pltpu.make_async_copy(mask_ref, masks.at[2], local_sem.at[1])

    def place(flip, row, d):
        e = d + row
        return e // 2 - 2, half(flip, row), half(flip, e % 2)

    def start(source, target, receiving, sending, to):
        copy = pltpu.make_async_remote_copy(
            src_ref=source,
            dst_ref=target,
            send_sem=send.at[sending],
            recv_sem=receiving,
            device_id=to,
            device_id_type=MESH,
        )
        copy.start()

    def landed(target, receiving):
        pltpu.make_async_remote_copy(
            src_ref=target,
            dst_ref=target,
            send_sem=send.at[0],
            recv_sem=receiving,
            device_id=slow,
            device_id_type=MESH,
        ).wait_recv()

    def sent(source, sending):
        pltpu.make_async_remote_copy(
            src_ref=source,
            dst_ref=source,
            send_sem=send.at[sending],
            recv_sem=near_sem.at[0],
            device_id=slow,
            device_id_type=MESH,
        ).wait_send()

    def give(source, at, flip, pieces, semaphores, number, sending, to):
        for i, piece in enumerate(pieces):
            part = span(flip, piece)
            start(source.at[part], held.at[at, part], semaphores.at[number + i], sending, to)

    def take(at, flip, pieces, semaphores, number):
        for i, piece in enumerate(pieces):
            landed(held.at[at, span(flip, piece)], semaphores.at[number + i])

    def give_mask(at, semaphore, side, to):
        start(mask_ref, masks.at[at], mask_sem.at[semaphore], side, to)

    pl.semaphore_wait(barrier, jnp.where(first, 1, jnp.where(last, 2, 2 - core)))

    @pl.when(core == 0)
    def _():
        pl.semaphore_signal(ready, inc=1, device_id=fast, device_id_type=MESH)

    @pl.when(last)
    def _():
        pl.semaphore_signal(ready, inc=1, device_id=slow, device_id_type=MESH)

    def give_slow():
        give_mask(1, 0, 0, slow)
        give(x_ref, 1, 1 - core, MOST, near_sem, 0, 2, slow)
        give_rest()

    def give_rest():
        give(x_ref, 1, 1 - core, NEAR[4], near_sem, 8, 2, slow)

    @pl.when(jnp.logical_not(jnp.logical_or(first, last)))
    def _():
        give_slow()

    @pl.when(last)
    def _():
        give_mask(4, 3, 0, (0, 1))
        for i, pieces in enumerate(FAR):
            give(x_ref, 4, 0, pieces, far_sem, PIECES + 2 * i, 2, (0, 1))
        give_rest()

    own.start()
    own_mask.start()

    @pl.when(core == 1)
    def _():
        pl.semaphore_wait(ready, 1)

    give_mask(3, 1, 1, fast)
    for i, pieces in enumerate(NEAR):
        give(x_ref, 3, core, pieces, near_sem, PIECES + 2 * i, 3, fast)

    @pl.when(first)
    def _():
        pl.semaphore_wait(ready, 1)
        give_slow()

    for j in range(3):
        for row, d, at, k in ((0, K, j, j + 2), (1, -1, j + 2, j)):
            _, r, c = place(core, row, d)
            high[at, k, r, c] = jnp.zeros((BLK, BLK), BF16)
            low[at, k, r, c] = jnp.zeros((BLK, BLK), BF16)
    cube[...] = jnp.zeros_like(cube)

    def mark(at):
        value = masks[at].astype(F32)
        for s in range(SLOTS):
            one = value[s // K : s // K + 1, s % K : s % K + 1]
            marks[at, s : s + 1, :] = jnp.broadcast_to(one, (1, BLK))

    def split(at, flip, pieces, turned=None):
        for row, first, count in pieces:
            def one(d, carry, row=row):
                s = entry(flip, row, d)
                k, r, c = place(flip, row, d)
                value = held[at, s] * marks[at, pl.ds(s, 1), :]
                top = value.astype(BF16)
                k = at + k if turned is None else turned(k)
                high[at, k, r, c] = top
                low[at, k, r, c] = (value - top.astype(F32)).astype(BF16)
                return carry

            if count < 3:
                for d in range(first, first + count):
                    one(d, 0)
            else:
                lax.fori_loop(first, first + count, one, 0)

    def square_row(j, tiles, fresh=False):
        for k in tiles:
            term = product(high[2, j], low[2, j], high[j, k], low[j, k])
            square[k] = term if fresh else square[k] + term

    def cube_row(j, tiles):
        for k in tiles:
            cube[k] = cube[k] + product(s_high[j], s_low[j], high[j, k], low[j, k])

    def finish_square(j, r=slice(None), c=slice(None)):
        value = square[j, r, c]
        top = value.astype(BF16)
        s_high[j, r, c] = top
        s_low[j, r, c] = (value - top.astype(F32)).astype(BF16)

    def give_out(flip, pieces, tile):
        for row, first, count in pieces:
            def one(d, carry, row=row):
                s = entry(flip, row, d)
                k, r, c = place(flip, row, d)
                k = tile(k + 2)
                value = 3.0 * square[k, r, c] - 2.0 * cube[k, r, c]
                out_ref[s] = value * marks[2, pl.ds(s, 1), :]
                return carry

            for d in range(first, first + count):
                one(d, 0)

    own.wait()
    own_mask.wait()
    mark(2)
    split(2, core, ((0, 0, K), (1, 0, K)))

    square_row(2, range(5), fresh=True)

    def pass_on(side, i=None):
        at, far, flip, other = (3, 0, 1 - core, slow) if side else (1, 4, core, fast)
        if i is None:
            start(masks.at[at], masks.at[far], mask_sem.at[3 - side], 4 + side, other)
        else:
            give(held.at[at], far, flip, FAR[i], far_sem, PIECES * (1 - side) + 2 * i, 6 + side, other)

    def near(side, i):
        at, flip = (3, 1 - core) if side else (1, core)
        take(at, flip, NEAR[i], near_sem, PIECES * side + 2 * i)
        if i < 4:
            pass_on(side, i)
        split(at, flip, NEAR[i], turned=(lambda k: 3 - k) if side else None)
        if i != 2:
            k = (3, 2, 1, 1, 0)[i]
            square_row(at, (4 - k if side else k,))

    for side in (1, 0):
        at = 3 if side else 1
        landed(masks.at[at], mask_sem.at[side])
        if side:
            pass_on(side)
        else:
            pl.when(jnp.logical_not(first))(lambda: pass_on(0))
        mark(at)
        if not side:
            take(1, core, MOST, near_sem, 0)

            @pl.when(jnp.logical_not(first))
            def _():
                for i in range(4):
                    pass_on(0, i)

            split(1, core, MOST)
            square_row(1, (3, 2, 1))
        for i in range(5) if side else (4,):
            near(side, i)

    for final in (False, True):
        side = jnp.where(second == final, 1, 0)
        flip = jnp.where(side == 0, core, 1 - core)

        def tile(k, side=side):
            return jnp.where(side == 0, k, 4 - k)

        far = tile(0)
        landed(masks.at[far], mask_sem.at[2 + side])
        if final:
            pl.when(second)(lambda: start(masks.at[4], masks.at[1], mask_sem.at[0], 8, fast))
        mark(far)
        for i, pieces in enumerate(FAR):
            take(far, flip, pieces, far_sem, PIECES * side + 2 * i)
            if final and i == 3:
                pl.when(second)(lambda: give(held.at[4], 1, 0, MOST, near_sem, 0, 9, fast))
            split(far, flip, pieces, turned=lambda k: tile(k))
            if i == 0:
                square_row(far, (2,))
                if final:
                    finish_square(2)
                    cube_row(2, range(5))
            elif i == 1:
                square_row(far, (tile(1),))
                finish_square(tile(1))
                cube_row(tile(1), [tile(k) for k in range(4)])
            elif i == 2:
                r0, r1 = half(flip, 0), half(flip, 1)
                c0, c1 = r0, r1
                everything = slice(None)
                square[far, :, c1] += product(high[2, far], low[2, far], high[far, far, :, c1], low[far, far, :, c1])
                finish_square(far, everything, c1)
                a_high, a_low = s_high[far, :, c1], s_low[far, :, c1]
                for k in (tile(1), tile(2)):
                    cube[k] += product(a_high, a_low, high[far, k, c1, :], low[far, k, c1, :])
                cube[far, :, c1] += product(a_high, a_low, high[far, far, c1, c1], low[far, far, c1, c1])
                if final:
                    give_out(flip, ((0, 5, 4), (1, 0, K)), tile)
            elif not final:
                square[far, r0, c0] += product(high[2, far, r0, :], low[2, far, r0, :], high[far, far, :, c0], low[far, far, :, c0])
                finish_square(far, r0, c0)
                a_high, a_low = s_high[far, r0, c0], s_low[far, r0, c0]
                cube[far, r0, c0] += product(s_high[far, r0, :], s_low[far, r0, :], high[far, far, :, c0], low[far, far, :, c0])
                cube[far, r0, c1] += product(a_high, a_low, high[far, far, c0, c1], low[far, far, c0, c1])
                k = tile(1)
                cube[k, r0, :] += product(a_high, a_low, high[far, k, c0, :], low[far, k, c0, :])
                cube[2, r0, c0] += product(a_high, a_low, high[far, 2, c0, c0], low[far, 2, c0, c0])

    def all_sent(first_sem, count):
        sent(masks.at[2], first_sem)
        sent(held.at[2, pl.ds(0, count)], first_sem + 1 if first_sem > 7 else first_sem + 2)

    all_sent(0, 15)
    all_sent(1, 15)
    all_sent(5, 11)
    pl.when(jnp.logical_not(first))(lambda: all_sent(4, 11))
    pl.when(second)(lambda: all_sent(8, 11))


def finish(cols, part_ref, marks, high, low, s_high, s_low, square, cube, out_ref, rest, sems):
    g = lax.axis_index("row") * cols + lax.axis_index("col")
    core, second = lax.rem(g, 2), g == 1
    flip = jnp.where(second, 1 - core, core)
    far, near = jnp.where(second, 4, 0), jnp.where(second, 3, 1)
    copies = []

    def write(source, target, n):
        copy = pltpu.make_async_copy(source, out_ref.at[target], sems.at[n])
        copy.start()
        copies.append(copy)

    for n, piece in enumerate(((1, 0, K), (0, 5, 4))):
        part = span(flip, piece)
        write(part_ref.at[part], part, n)

    r0, c0, c1 = half(flip, 0), half(flip, 0), half(flip, 1)

    def times(a, j, k, r, c):
        return product(*a, high[j, k, r, c], low[j, k, r, c])

    def put(d, at, s_block, c_block):
        mark = marks[2, pl.ds(entry(flip, 0, d), 1), :]
        rest[at] = (3.0 * s_block - 2.0 * c_block) * mark

    whole = slice(None)
    corner = square[far, r0, c0] + times((high[2, far, r0, :], low[2, far, r0, :]), far, far, whole, c0)
    top = corner.astype(BF16)
    left = top, (corner - top.astype(F32)).astype(BF16)
    beside = s_high[far, r0, c1], s_low[far, r0, c1]

    def at(d):
        return jnp.where(flip == 0, d, 4 - d)

    put(0, at(0), corner, cube[far, r0, c0] + times(left, far, far, c0, c0) + times(beside, far, far, c1, c0))
    put(1, at(1), square[far, r0, c1], cube[far, r0, c1] + times(left, far, far, c0, c1))
    both = cube[near, r0, :] + times(left, far, near, c0, whole)
    for h in range(2):
        columns = slice(h * BLK, (h + 1) * BLK)
        d = jnp.where(flip == 0, 2 + h, 3 - h)
        put(d, at(d), square[near, r0, columns], both[:, columns])
    put(4, at(4), square[2, r0, c0], cube[2, r0, c0] + times(left, far, 2, c0, c0))

    write(rest, span(flip, (0, 0, 5)), 2)
    for copy in copies:
        copy.wait()


def solution(mesh):
    rows, cols = mesh.shape["row"], mesh.shape["col"]

    def local(density, band_mask):
        blocks = pltpu.with_memory_space_constraint(
            density.reshape(SLOTS, BLK, BLK), pltpu.HBM
        )
        mask = pltpu.with_memory_space_constraint(band_mask, pltpu.HBM)
        tiles, line = (5, 5, TILE, TILE), (5, TILE, TILE)
        blocks_shape = jax.ShapeDtypeStruct((SLOTS, BLK, BLK), F32)
        vmem = pl.BlockSpec(memory_space=pltpu.VMEM)
        parts = pl.pallas_call(
            functools.partial(kernel, rows, cols),
            out_shape=[
                blocks_shape,
                jax.ShapeDtypeStruct((5, 24, BLK), F32),
                jax.ShapeDtypeStruct(tiles, BF16),
                jax.ShapeDtypeStruct(tiles, BF16),
                jax.ShapeDtypeStruct(line, BF16),
                jax.ShapeDtypeStruct(line, BF16),
                jax.ShapeDtypeStruct(line, F32),
                jax.ShapeDtypeStruct(line, F32),
            ],
            in_specs=[
                pl.BlockSpec(memory_space=pltpu.HBM),
                pl.BlockSpec(memory_space=pltpu.HBM),
            ],
            out_specs=[vmem] * 8,
            scratch_shapes=[
                pltpu.VMEM((5, SLOTS, BLK, BLK), F32),
                pltpu.VMEM((5, 2, K), jnp.int32),
                pltpu.SemaphoreType.DMA((10,)),
                pltpu.SemaphoreType.DMA((4,)),
                pltpu.SemaphoreType.DMA((2 * PIECES,)),
                pltpu.SemaphoreType.DMA((2 * PIECES,)),
                pltpu.SemaphoreType.DMA((2,)),
                pltpu.SemaphoreType.REGULAR,
            ],
            compiler_params=pltpu.CompilerParams(
                collective_id=0, has_side_effects=True, vmem_limit_bytes=24 << 20
            ),
        )(blocks, mask)
        result = pl.pallas_call(
            functools.partial(finish, cols),
            out_shape=blocks_shape,
            in_specs=[vmem] * 8,
            out_specs=pl.BlockSpec(memory_space=pltpu.HBM),
            scratch_shapes=[
                pltpu.VMEM((5, BLK, BLK), F32),
                pltpu.SemaphoreType.DMA((3,)),
            ],
            compiler_params=pltpu.CompilerParams(vmem_limit_bytes=4 << 20),
        )(*parts)
        return result.reshape(density.shape)

    return jax.shard_map(
        local,
        mesh=mesh,
        in_specs=(P(("row", "col"), None, None, None), P(("row", "col"), None)),
        out_specs=P(("row", "col"), None, None, None),
        check_vma=False,
    )
```
